1024 devices in a mesh: dp: 64 (over y, x), tensor: 16 (over z, core).
Axes of the slice: x: 8, y: 8, z: 8, core: 2. Of those that a mesh axis runs over, the one named last changes fastest.
Arguments:
- activations: bfloat16 [8192, 4096], P('dp'), may hold values from -6 to 6
- out_grads: bfloat16 [8192, 28672], P('dp', 'tensor'), may hold values from -1536 to 1536
- token_ids: int32 [8192], P('dp'), may hold values from 0 to 128255, as said below
- prev_acts: bfloat16 [8192, 4096], P('dp'), may hold values from -6 to 6
- prev_grads: bfloat16 [8192, 28672], P('dp', 'tensor'), may hold values from -1536 to 1536
- prev_basis: float32 [4096, 32], replicated, may hold values from -0.09375 to 0.09375
- warm_start: float32 [28672, 32], P('tensor'), may hold values from -18 to 18
Outputs:
- update_rows: bfloat16 [4096, 28672], P('dp', 'tensor')
- next_start: float32 [28672, 32], P('tensor')
The draws below stay inside these ranges and needn't reach their ends.
Inputs may be any that keep to these rules, and one draw needn't show every extreme that they name: `token_ids`: each replica's block of 128 ids ends in 0 to 64 padding ids 0; the other ids are 1 or more.
All inputs are finite; a program needn't handle non-finite values.
Results may differ from the reference program's by a relative error of at most 0.0017.
Values sent between devices are 32-bit elements; how exact they have to be, the bound alone decides.
A program may use at most 32 MiB of HBM per device.

```python
import jax
import jax.numpy as jnp
from jax import lax

D = 4096
F = 28672
VOCAB = 128256
R = 32
TOK_DEV = 128
TOKENS = 8192
N_DP = 64


def draw_token_ids(key, part):
    key = jax.random.fold_in(key, 7)
    key_ids, key_pads = jax.random.split(key)
    blocks = TOKENS // TOK_DEV
    raw_ids = jax.random.randint(key_ids, (TOKENS,), 1, VOCAB)
    padding = jax.random.randint(key_pads, (blocks,), 0, TOK_DEV // 2 + 1)
    places = jnp.arange(TOKENS)
    within = places % TOK_DEV
    owner = places // TOK_DEV
    return jnp.where(within >= TOK_DEV - padding[owner], 0, raw_ids).astype(jnp.int32)


def shard_levels(key, dims, shards, low, largest):
    factor_of, own = 1.0, jax.random.fold_in(key, 6)
    for dim, blocks in shards:
        heights = jnp.exp(jax.random.uniform(jax.random.fold_in(own, dim), (blocks,), jnp.float32, low / len(shards), largest / len(shards)))
        factor_of = factor_of * jnp.repeat(heights, dims[dim] // blocks).reshape([-1 if axis == dim else 1 for axis in range(len(dims))])
    return factor_of


def noise(rng, dims, scale, reach, cuts=(), kind=jnp.bfloat16):
    drawn = scale * jax.random.normal(rng, dims, jnp.float32)
    if cuts:
        drawn = drawn * shard_levels(rng, dims, cuts, -0.22, 0.18)
    return jnp.clip(drawn, -reach, reach).astype(kind)


def setup_inputs(seed: int = 0) -> dict:
    key_list = jax.random.split(jax.random.key(seed), 8)
    activations = noise(key_list[0], (TOKENS, D), 1.0, 6.0, ((0, 64),))
    out_grads = noise(key_list[1], (TOKENS, F), 256.0, 1536.0, ((0, 64), (1, 16)))
    token_ids = draw_token_ids(jax.random.fold_in(key_list[7], 71), 0)
    prev_acts = noise(key_list[3], (TOKENS, D), 1.0, 6.0, ((0, 64),))
    prev_grads = noise(key_list[4], (TOKENS, F), 256.0, 1536.0, ((0, 64), (1, 16)))
    prev_basis = noise(key_list[5], (D, R), D ** -0.5, 0.09375, (), jnp.float32)
    warm_start = noise(key_list[6], (F, R), 3.0, 18.0, ((0, 16),), jnp.float32)
    return {"activations": activations, "out_grads": out_grads, "token_ids": token_ids, "prev_acts": prev_acts, "prev_grads": prev_grads, "prev_basis": prev_basis, "warm_start": warm_start}


def orthonormal(left):
    highest = lax.Precision.HIGHEST
    square = jnp.dot(left.T.astype(jnp.float32), left.astype(jnp.float32), precision=highest, preferred_element_type=jnp.float32)
    factor = jnp.linalg.cholesky(square)
    return jax.scipy.linalg.solve_triangular(factor, left.T, lower=True).T

def reference(activations, out_grads, token_ids, prev_acts, prev_grads, prev_basis, warm_start):
    highest = lax.Precision.HIGHEST
    inputs = activations.astype(jnp.float32).reshape(N_DP, TOK_DEV, D)
    grads = out_grads.astype(jnp.float32).reshape(N_DP, TOK_DEV, F)
    old_inputs = prev_acts.astype(jnp.float32).reshape(N_DP, TOK_DEV, D)
    old_grads = prev_grads.astype(jnp.float32).reshape(N_DP, TOK_DEV, F)
    token_mask = (token_ids != 0).astype(jnp.float32).reshape(N_DP, TOK_DEV, 1)
    live = jnp.sum(token_mask)
    inv_tokens = 1.0 / (N_DP * TOK_DEV)
    proj_now = jnp.einsum('ntf,fr->ntr', grads, warm_start, precision=highest) * token_mask
    proj_old = jnp.einsum('ntf,fr->ntr', old_grads, warm_start, precision=highest)
    warm_gram = jnp.dot(warm_start.T.astype(jnp.float32), warm_start.astype(jnp.float32), precision=highest, preferred_element_type=jnp.float32)
    part_now = jnp.einsum('ntd,ntr->dr', inputs, proj_now, precision=highest)
    part_old = jnp.einsum('ntd,ntr->dr', old_inputs, proj_old, precision=highest) * inv_tokens
    left = part_now / live + part_old - jnp.dot(prev_basis.astype(jnp.float32), warm_gram.astype(jnp.float32), precision=highest, preferred_element_type=jnp.float32)
    basis = orthonormal(left)
    back_now = jnp.einsum('ntd,dr->ntr', inputs, basis, precision=highest) * token_mask
    back_old = jnp.einsum('ntd,dr->ntr', old_inputs, basis, precision=highest)
    cross = jnp.dot(prev_basis.T.astype(jnp.float32), basis.astype(jnp.float32), precision=highest, preferred_element_type=jnp.float32)
    next_start = jnp.einsum('ntf,ntr->fr', grads, back_now, precision=highest) / live + jnp.einsum('ntf,ntr->fr', old_grads, back_old, precision=highest) * inv_tokens - jnp.dot(warm_start.astype(jnp.float32), cross.astype(jnp.float32), precision=highest, preferred_element_type=jnp.float32)
    update_rows = jnp.dot(basis.astype(jnp.float32), next_start.T.astype(jnp.float32), precision=highest, preferred_element_type=jnp.float32).astype(jnp.bfloat16)
    return (update_rows, next_start)
```

```python
import jax
import jax.numpy as jnp
from jax import lax
from jax.experimental import pallas as pl
from jax.experimental.pallas import tpu as pltpu
from jax.sharding import PartitionSpec as P

MESH = pl.DeviceIdType.MESH
F32, BF16 = jnp.float32, jnp.bfloat16
HIGHEST = lax.Precision.HIGHEST

SIDE = 8
NT = 16
REPLICAS = 64
TOK = 128
RANK = 32
OWN = RANK // NT
DIM = 4096
FF = 1792
DCH = DIM // SIDE
FAR = (4, 3, 5, 2, 6, 1, 7)
INV_TOKENS = 1.0 / (REPLICAS * TOK)
ACOLS = 1024
BCOLS = 384


def nt_dot(first, second):
    return lax.dot_general(first, second, (((1,), (1,)), ((), ())), preferred_element_type=F32)


def dot32(first, second, dims=((1,), (0,))):
    return lax.dot_general(first, second, (dims, ((), ())), precision=HIGHEST, preferred_element_type=F32)


def pieces(value):
    high = value.astype(BF16).astype(F32)
    rest = value - high
    mid = rest.astype(BF16).astype(F32)
    low = (rest - mid).astype(BF16).astype(F32)
    return high, mid, low


def total(ref, count):
    acc = ref[0]
    for k in range(1, count):
        acc = acc + ref[k]
    return acc


def inverse_factor(gram):
    rows = lax.broadcasted_iota(jnp.int32, (RANK, 128), 0)
    lanes = lax.broadcasted_iota(jnp.int32, (RANK, 128), 1)
    eye = (lanes == rows + RANK).astype(F32)
    work = jnp.concatenate([gram, jnp.zeros((RANK, 128 - RANK), F32)], axis=1) + eye
    for k in range(RANK):
        row = work[k : k + 1, :]
        pivot = row[:, k : k + 1]
        column = work[:, k : k + 1]
        scaled = row * (1.0 / pivot)
        root = row * lax.rsqrt(pivot)
        below = work - column * scaled
        work = jnp.where(rows > k, below, jnp.where(rows == k, root, work))
    return work[:, RANK : 2 * RANK]


def kernel(
    x_hbm, y_hbm, ids_ref, u_hbm, v_hbm, bt_hbm, wt_hbm,
    upd_ref, nxt_ref,
    xub, yvw, bt, wt,
    a_send, a_recv, l_send, l_recv, b_send, b_recv, c_send, c_recv, d_send, d_recv,
    gb, lf, g_send, g_recv, back, mine, crs, cw,
    ea_send, ea_recv, eb_send, eb_recv, fa_send, fa_recv, fb_send, fb_recv,
    ga_send, ga_recv, gb_send, gb_recv,
    load_sem, send_sem, recv_sem,
):
    dp, t = lax.axis_index("dp"), lax.axis_index("tensor")
    y, x = dp // SIDE, lax.rem(dp, SIDE)
    z, core = t // 2, lax.rem(t, 2)

    loads = []
    for k, (src, dst) in enumerate(
        (
            (wt_hbm, wt),
            (y_hbm, yvw.at[pl.ds(0, TOK)]),
            (v_hbm, yvw.at[pl.ds(TOK, TOK)]),
            (bt_hbm, bt),
            (x_hbm, xub.at[pl.ds(0, TOK)]),
            (u_hbm, xub.at[pl.ds(TOK, TOK)]),
        )
    ):
        copy = pltpu.make_async_copy(src, dst, load_sem.at[k])
        copy.start()
        loads.append(copy)

    ring = [lax.rem(jnp.int32(k) + x, SIDE) for k in FAR]
    xs = [(k, (y * SIDE + k, t)) for k in ring]
    ring = [lax.rem(jnp.int32(k) + y, SIDE) for k in FAR]
    ys = [(k, (k * SIDE + x, t)) for k in ring]
    ts = []
    for k in FAR:
        zk = lax.rem(z + k, SIDE)
        ts += [(zk * 2, (dp, zk * 2)), (zk * 2 + 1, (dp, zk * 2 + 1))]
    ts.append((t + 1 - 2 * core, (dp, t + 1 - 2 * core)))

    barrier = pltpu.get_barrier_semaphore()
    for _, peer in ts + ys + xs:
        pl.semaphore_signal(barrier, inc=1, device_id=peer, device_id_type=MESH)

    def send(phase, src, dst, peer):
        pltpu.make_async_remote_copy(
            src_ref=src, dst_ref=dst, send_sem=send_sem.at[phase], recv_sem=recv_sem.at[phase], device_id=peer, device_id_type=MESH
        ).start()

    def arrived(phase, ref, count):
        whole = ref.at[pl.ds(0, count)]
        pltpu.make_async_copy(whole, whole, recv_sem.at[phase]).wait()

    def left(phase, ref, count):
        whole = ref.at[pl.ds(0, count)]
        pltpu.make_async_copy(whole, whole, send_sem.at[phase]).wait()

    mask = (ids_ref[...] != 0).astype(F32)
    l_send[...] = jnp.broadcast_to(jnp.sum(mask, axis=1, keepdims=True), (1, 128))
    loads[0].wait()
    for k, piece in enumerate(pieces(wt[...])):
        yvw[2 * TOK + k * RANK : 2 * TOK + (k + 1) * RANK, :] = piece.astype(BF16)
    yvw[2 * TOK + 3 * RANK :, :] = jnp.zeros((RANK, FF), BF16)
    loads[1].wait()
    loads[2].wait()
    proj = nt_dot(yvw[2 * TOK : 2 * TOK + 3 * RANK, :], yvw[...])
    proj = proj[:RANK] + proj[RANK : 2 * RANK] + proj[2 * RANK :]
    for k in range(NT):
        own = proj[OWN * k : OWN * (k + 1)]
        a_send[k] = jnp.concatenate([own[:, :128], own[:, 128:256], own[:, 256:], own[:, 256:]], axis=0)
    pl.semaphore_wait(barrier, len(ts + ys + xs))

    for k, peer in ts:
        send(0, a_send.at[k], a_recv.at[t], peer)
    for _, peer in xs:
        send(1, l_send, l_recv.at[x], peer)
    a_recv[t] = a_send[t]
    l_recv[x] = l_send[...]
    loads[3].wait()
    for k, piece in enumerate(pieces(bt[...])):
        xub[2 * TOK + k * RANK : 2 * TOK + (k + 1) * RANK, :] = piece.astype(BF16)
    xub[2 * TOK + 3 * RANK :, :] = jnp.zeros((RANK, DIM), BF16)
    loads[4].wait()
    loads[5].wait()
    arrived(0, a_recv, NT - 1)
    own = total(a_recv, NT)
    rows = lax.broadcasted_iota(jnp.int32, (2 * OWN, TOK), 0)
    now = jnp.where(rows < OWN, own[: 2 * OWN] * mask, 0.0)
    old = jnp.where(rows >= OWN, own[: 2 * OWN] * INV_TOKENS, 0.0)
    stacked = jnp.concatenate([now, old], axis=1)
    stacked = jnp.concatenate([*pieces(stacked), jnp.zeros((2 * OWN, 2 * TOK), F32)], axis=0).astype(BF16)
    arrived(1, l_recv, SIDE - 1)
    live_x = jnp.broadcast_to(total(l_recv, SIDE), (2 * OWN, 128))

    def left_chunk(k):
        part = jnp.dot(stacked, xub[: 2 * TOK, pl.ds(pl.multiple_of(k * DCH, DCH), DCH)], preferred_element_type=F32)
        return part[: 2 * OWN] + part[2 * OWN : 4 * OWN] + part[4 * OWN : 6 * OWN]

    for k, peer in ys:
        b_send[k, :, :DCH] = left_chunk(k)
        b_send[k, :, DCH:] = live_x
        send(2, b_send.at[k], b_recv.at[y], peer)
    b_recv[y, :, :DCH] = left_chunk(y)
    b_recv[y, :, DCH:] = live_x
    square = own[4:6, :RANK] + own[4:6, RANK : 2 * RANK] + own[4:6, 2 * RANK : 3 * RANK]
    gb[...] = dot32(square, bt[...])
    arrived(2, b_recv, SIDE - 1)
    summed = total(b_recv, SIDE)
    inv_live = 1.0 / summed[:1, DCH : DCH + 128]
    inv_wide = jnp.concatenate([inv_live] * (DCH // 128), axis=1)
    chunk = summed[:OWN, :DCH] * inv_wide + summed[OWN:, :DCH]
    c_send[...] = chunk
    for _, peer in xs:
        send(3, c_send, c_recv.at[x], peer)
    c_recv[x] = chunk
    arrived(3, c_recv, SIDE - 1)

    chunk = total(c_recv, SIDE)
    d_send[...] = chunk
    for _, peer in ys:
        send(4, d_send, d_recv.at[y], peer)
    d_recv[y] = chunk
    arrived(4, d_recv, SIDE - 1)
    acc = jnp.zeros((16, 3 * 128), F32)
    for k in range(SIDE):
        part = d_recv[k] - gb[:, k * DCH : (k + 1) * DCH]
        lf[:, k * DCH : (k + 1) * DCH] = part
        part = jnp.concatenate([*pieces(part), jnp.zeros((16 - 3 * OWN, DCH), F32)], axis=0).astype(BF16)
        acc = acc + nt_dot(part, xub[:, k * DCH : (k + 1) * DCH])
    acc = acc[:OWN] + acc[OWN : 2 * OWN] + acc[2 * OWN : 3 * OWN]

    my_lanes = pl.ds(pl.multiple_of(dp // 2 * 128, 128), 128)
    tile = jnp.concatenate(
        [acc[:, :128] * (mask * inv_live), acc[:, 128:256] * INV_TOKENS, lf[:, my_lanes], acc[:, 256:]], axis=0
    )
    g_send[...] = tile
    for _, peer in ts:
        send(5, g_send, g_recv.at[t], peer)
    g_recv[t] = tile
    arrived(5, g_recv, NT - 1)
    for k in range(NT):
        tile = g_recv[k]
        at = slice(OWN * k, OWN * (k + 1))
        back[at, :128] = tile[:2]
        back[at, 128:] = tile[2:4]
        mine[at, :] = tile[4:6]
        crs[at, :] = tile[6:8]

    stacked = jnp.concatenate(pieces(back[...]), axis=0).astype(BF16)

    def right_part(first, width):
        part = jnp.dot(stacked, yvw[: 2 * TOK, pl.ds(first, width)], preferred_element_type=F32)
        return part[:RANK] + part[RANK : 2 * RANK] + part[2 * RANK :]

    for k in range(0, SIDE, 2):
        part = right_part(k * 128, 256)
        ea_send[k] = part[:, :128]
        ea_send[k + 1] = part[:, 128:]
    for k, peer in ys:
        send(6, ea_send.at[k], ea_recv.at[y], peer)
    half = lax.rem(dp, 2)
    lanes = lax.broadcasted_iota(jnp.int32, (RANK, 128), 1)
    my_rows = jnp.where(lanes // 64 == half, mine[...], 0.0)
    gram = dot32(my_rows, my_rows, ((1,), (1,)))
    gram = jnp.concatenate([gram[8 * k : 8 * (k + 1)] for k in range(RANK // 8)], axis=1)
    for h in range(2):
        part = right_part(ACOLS + h * BCOLS, BCOLS)
        for k in range(RANK // 8):
            eb_send[2 * k + h, :, :BCOLS] = part[8 * k : 8 * (k + 1)]
            eb_send[2 * k + h, :, BCOLS:] = gram
    for k, peer in xs:
        send(7, eb_send.at[k], eb_recv.at[x], peer)
    ea_recv[y] = ea_send[y]
    eb_recv[x] = eb_send[x]
    cross = crs[:, :RANK] + crs[:, RANK : 2 * RANK] + crs[:, 2 * RANK : 3 * RANK]
    cw[...] = dot32(cross, wt[...])
    arrived(6, ea_recv, SIDE - 1)
    part = total(ea_recv, SIDE)
    fa_send[...] = part
    for _, peer in xs:
        send(8, fa_send, fa_recv.at[x], peer)
    fa_recv[x] = part
    arrived(7, eb_recv, SIDE - 1)
    part = total(eb_recv, SIDE)
    fb_send[...] = part
    for _, peer in ys:
        send(9, fb_send, fb_recv.at[y], peer)
    fb_recv[y] = part
    arrived(8, fa_recv, SIDE - 1)
    part = total(fa_recv, SIDE)
    ga_send[...] = part
    for _, peer in ys:
        send(10, ga_send, ga_recv.at[y], peer)
    ga_recv[y] = part
    arrived(9, fb_recv, SIDE - 1)
    part = total(fb_recv, SIDE)
    gb_send[...] = part[:, :BCOLS]
    for _, peer in xs:
        send(11, gb_send, gb_recv.at[x], peer)
    gb_recv[x] = part[:, :BCOLS]
    packed = part[:, BCOLS:]
    gram = jnp.concatenate([packed[:, RANK * k : RANK * (k + 1)] for k in range(RANK // 8)], axis=0)
    inverse = inverse_factor(gram)
    basis = dot32(inverse, mine[...])
    rows = dot32(basis, inverse, ((0,), (0,)))
    rows = jnp.where(half == 0, rows[:64], rows[64:])
    both = jnp.concatenate([inverse, rows], axis=0)

    def finish(first, raw):
        width = raw.shape[1]
        out = dot32(both, raw - cw[:, first : first + width])
        nxt_ref[:, first : first + width] = out[:RANK]
        upd_ref[:, first : first + width] = out[RANK:].astype(BF16)

    arrived(10, ga_recv, SIDE - 1)
    for k in range(0, SIDE, 2):
        finish(k * 128, jnp.concatenate([ga_recv[k], ga_recv[k + 1]], axis=1))
    arrived(11, gb_recv, SIDE - 1)
    for h in range(2):
        finish(ACOLS + h * BCOLS, jnp.concatenate([gb_recv[2 * k + h] for k in range(RANK // 8)], axis=0))

    for phase, (ref, count) in enumerate(
        (
            (a_recv, NT - 1), (l_recv, SIDE - 1), (b_recv, SIDE - 1), (c_recv, SIDE - 1), (d_recv, SIDE - 1), (g_recv, NT - 1),
            (ea_recv, SIDE - 1), (eb_recv, SIDE - 1), (fa_recv, SIDE - 1), (fb_recv, SIDE - 1), (ga_recv, SIDE - 1), (gb_recv, SIDE - 1),
        )
    ):
        left(phase, ref, count)


def shards(activations, out_grads, token_ids, prev_acts, prev_grads, prev_basis, warm_start):
    def vmem(*shape, dtype=F32):
        return pltpu.VMEM(shape, dtype)

    hbm = pl.BlockSpec(memory_space=pl.ANY)
    local = pl.BlockSpec(memory_space=pltpu.VMEM)
    update, start = pl.pallas_call(
        kernel,
        out_shape=(jax.ShapeDtypeStruct((DIM // REPLICAS, FF), BF16), jax.ShapeDtypeStruct((RANK, FF), F32)),
        in_specs=[hbm, hbm, local, hbm, hbm, hbm, hbm],
        out_specs=(local, local),
        scratch_shapes=[
            vmem(3 * TOK, DIM, dtype=BF16), vmem(3 * TOK, FF, dtype=BF16), vmem(RANK, DIM), vmem(RANK, FF),
            vmem(NT, 8, 128), vmem(NT, 8, 128), vmem(1, 128), vmem(SIDE, 1, 128),
            vmem(SIDE, 2 * OWN, DCH + 128), vmem(SIDE, 2 * OWN, DCH + 128),
            vmem(OWN, DCH), vmem(SIDE, OWN, DCH), vmem(OWN, DCH), vmem(SIDE, OWN, DCH),
            vmem(OWN, DIM), vmem(OWN, DIM), vmem(8, 128), vmem(NT, 8, 128),
            vmem(RANK, 2 * TOK), vmem(RANK, 128), vmem(RANK, 128), vmem(RANK, FF),
            vmem(SIDE, RANK, 128), vmem(SIDE, RANK, 128), vmem(SIDE, 8, BCOLS + 128), vmem(SIDE, 8, BCOLS + 128),
            vmem(RANK, 128), vmem(SIDE, RANK, 128), vmem(8, BCOLS + 128), vmem(SIDE, 8, BCOLS + 128),
            vmem(RANK, 128), vmem(SIDE, RANK, 128), vmem(8, BCOLS), vmem(SIDE, 8, BCOLS),
            pltpu.SemaphoreType.DMA((6,)), pltpu.SemaphoreType.DMA((12,)), pltpu.SemaphoreType.DMA((12,)),
        ],
        compiler_params=pltpu.CompilerParams(collective_id=0, has_side_effects=True, vmem_limit_bytes=40 * 2**20),
        cost_estimate=pl.CostEstimate(flops=10**9, bytes_accessed=5 * 10**6, transcendentals=0),
    )(
        activations, out_grads, token_ids.reshape(1, TOK), prev_acts, prev_grads, prev_basis.T, warm_start.T
    )
    return update, start.T


def solution(mesh):
    in_specs = (P("dp", None), P("dp", "tensor"), P("dp"), P("dp", None), P("dp", "tensor"), P(), P("tensor", None))
    out_specs = (P("dp", "tensor"), P("tensor", None))
    return jax.shard_map(shards, mesh=mesh, in_specs=in_specs, out_specs=out_specs, check_vma=False)
```

```python
import jax
import jax.numpy as jnp
from jax import lax
from jax.experimental import pallas as pl
from jax.experimental.pallas import tpu as pltpu
from jax.sharding import PartitionSpec as P

MESH = pl.DeviceIdType.MESH
F32, BF16 = jnp.float32, jnp.bfloat16
HIGHEST = lax.Precision.HIGHEST

SIDE = 8
NT = 16
REPLICAS = 64
TOK = 128
RANK = 32
OWN = RANK // NT
DIM = 4096
FF = 1792
DCH = DIM // SIDE
FAR = (4, 3, 5, 2, 6, 1, 7)
INV_TOKENS = 1.0 / (REPLICAS * TOK)
ACOLS = 1024
BCOLS = 384


def nt_dot(first, second):
    return lax.dot_general(first, second, (((1,), (1,)), ((), ())), preferred_element_type=F32)


def dot32(first, second, dims=((1,), (0,))):
    return lax.dot_general(first, second, (dims, ((), ())), precision=HIGHEST, preferred_element_type=F32)


def pieces(value):
    high = value.astype(BF16).astype(F32)
    rest = value - high
    mid = rest.astype(BF16).astype(F32)
    low = (rest - mid).astype(BF16).astype(F32)
    return high, mid, low


def total(ref, count):
    acc = ref[0]
    for k in range(1, count):
        acc = acc + ref[k]
    return acc


def inverse_factor(gram):
    rows = lax.broadcasted_iota(jnp.int32, (RANK, 128), 0)
    lanes = lax.broadcasted_iota(jnp.int32, (RANK, 128), 1)
    eye = (lanes == rows + RANK).astype(F32)
    work = jnp.concatenate([gram, jnp.zeros((RANK, 128 - RANK), F32)], axis=1) + eye
    for k in range(RANK):
        row = work[k : k + 1, :]
        pivot = row[:, k : k + 1]
        column = work[:, k : k + 1]
        scaled = row * (1.0 / pivot)
        root = row * lax.rsqrt(pivot)
        below = work - column * scaled
        work = jnp.where(rows > k, below, jnp.where(rows == k, root, work))
    return work[:, RANK : 2 * RANK]


def kernel(
    x_hbm, y_hbm, ids_hbm, u_hbm, v_hbm, bt_hbm, wt_hbm,
    upd_ref, nxt_ref,
    xub, yvw, bt, wt,
    a_send, a_recv, l_send, l_recv, b_send, b_recv, c_send, c_recv, d_send, d_recv,
    gb, lf, g_send, g_recv, back, mine, crs, cw,
    ea_send, ea_recv, eb_send, eb_recv, fa_send, fa_recv, fb_send, fb_recv,
    ga_send, ga_recv, gb_send, gb_recv,
    h_send, h_recv, p_send, p_recv, q_send, q_recv, lp,
    ids, load_sem, send_sem, recv_sem, slot_sem,
):
    dp, t = lax.axis_index("dp"), lax.axis_index("tensor")
    y, x = dp // SIDE, lax.rem(dp, SIDE)
    z, core = t // 2, lax.rem(t, 2)

    ring = [lax.rem(jnp.int32(k) + x, SIDE) for k in FAR]
    xs = [(k, (y * SIDE + k, t)) for k in ring]
    ring = [lax.rem(jnp.int32(k) + y, SIDE) for k in FAR]
    ys = [(k, (k * SIDE + x, t)) for k in ring]
    ts = []
    for k in FAR:
        zk = lax.rem(z + k, SIDE)
        ts += [(zk * 2, (dp, zk * 2)), (zk * 2 + 1, (dp, zk * 2 + 1))]
    ts.append((t + 1 - 2 * core, (dp, t + 1 - 2 * core)))

    barrier = pltpu.get_barrier_semaphore()
    for _, peer in ts + ys + xs:
        pl.semaphore_signal(barrier, inc=1, device_id=peer, device_id_type=MESH)

    loads = []
    for k, (src, dst) in enumerate(
        (
            (wt_hbm, wt),
            (y_hbm, yvw.at[pl.ds(0, TOK)]),
            (v_hbm, yvw.at[pl.ds(TOK, TOK)]),
            (bt_hbm, bt),
            (x_hbm, xub.at[pl.ds(0, TOK)]),
            (u_hbm, xub.at[pl.ds(TOK, TOK)]),
            (ids_hbm, ids),
        )
    ):
        copy = pltpu.make_async_copy(src, dst, load_sem.at[k])
        copy.start()
        loads.append(copy)

    def send(phase, src, dst, peer, sem=None):
        sem = recv_sem.at[phase] if sem is None else sem
        pltpu.make_async_remote_copy(
            src_ref=src, dst_ref=dst, send_sem=send_sem.at[phase], recv_sem=sem, device_id=peer, device_id_type=MESH
        ).start()

    def arrived(phase, ref, count):
        whole = ref.at[pl.ds(0, count)]
        pltpu.make_async_copy(whole, whole, recv_sem.at[phase]).wait()

    def left(phase, ref, count):
        whole = ref.at[pl.ds(0, count)]
        pltpu.make_async_copy(whole, whole, send_sem.at[phase]).wait()

    loads[6].wait()
    mask = (ids[...] != 0).astype(F32)
    l_send[...] = jnp.broadcast_to(jnp.sum(mask, axis=1, keepdims=True), (1, 128))
    loads[0].wait()
    for k, piece in enumerate(pieces(wt[...])):
        yvw[2 * TOK + k * RANK : 2 * TOK + (k + 1) * RANK, :] = piece.astype(BF16)
    yvw[2 * TOK + 3 * RANK :, :] = jnp.zeros((RANK, FF), BF16)
    loads[1].wait()
    loads[2].wait()
    proj = nt_dot(yvw[2 * TOK : 2 * TOK + 3 * RANK, :], yvw[...])
    proj = proj[:RANK] + proj[RANK : 2 * RANK] + proj[2 * RANK :]
    for k in range(NT):
        own = proj[OWN * k : OWN * (k + 1)]
        a_send[k] = jnp.concatenate([own[:, :128], own[:, 128:256], own[:, 256:], own[:, 256:]], axis=0)
    pl.semaphore_wait(barrier, len(ts + ys + xs))

    for k, peer in ts:
        send(0, a_send.at[k], a_recv.at[t], peer)
    for _, peer in xs:
        send(1, l_send, l_recv.at[x], peer)
    a_recv[t] = a_send[t]
    l_recv[x] = l_send[...]
    loads[3].wait()
    for k, piece in enumerate(pieces(bt[...])):
        xub[2 * TOK + k * RANK : 2 * TOK + (k + 1) * RANK, :] = piece.astype(BF16)
    xub[2 * TOK + 3 * RANK :, :] = jnp.zeros((RANK, DIM), BF16)
    loads[4].wait()
    loads[5].wait()
    arrived(0, a_recv, NT - 1)
    own = total(a_recv, NT)
    rows = lax.broadcasted_iota(jnp.int32, (2 * OWN, TOK), 0)
    now = jnp.where(rows < OWN, own[: 2 * OWN] * mask, 0.0)
    old = jnp.where(rows >= OWN, own[: 2 * OWN] * INV_TOKENS, 0.0)
    stacked = jnp.concatenate([now, old], axis=1)
    stacked = jnp.concatenate([*pieces(stacked), jnp.zeros((2 * OWN, 2 * TOK), F32)], axis=0).astype(BF16)
    arrived(1, l_recv, SIDE - 1)
    live_x = jnp.broadcast_to(total(l_recv, SIDE), (2 * OWN, 128))

    def left_chunk(k):
        part = jnp.dot(stacked, xub[: 2 * TOK, pl.ds(pl.multiple_of(k * DCH, DCH), DCH)], preferred_element_type=F32)
        return part[: 2 * OWN] + part[2 * OWN : 4 * OWN] + part[4 * OWN : 6 * OWN]

    for k, peer in ys:
        b_send[k, :, :DCH] = left_chunk(k)
        b_send[k, :, DCH:] = live_x
        send(2, b_send.at[k], b_recv.at[y], peer)
    b_recv[y, :, :DCH] = left_chunk(y)
    b_recv[y, :, DCH:] = live_x
    square = own[4:6, :RANK] + own[4:6, RANK : 2 * RANK] + own[4:6, 2 * RANK : 3 * RANK]
    gb[...] = dot32(square, bt[...])
    arrived(2, b_recv, SIDE - 1)
    summed = total(b_recv, SIDE)
    inv_live = 1.0 / summed[:1, DCH : DCH + 128]
    inv_wide = jnp.concatenate([inv_live] * (DCH // 128), axis=1)
    chunk = summed[:OWN, :DCH] * inv_wide + summed[OWN:, :DCH]
    c_send[...] = chunk
    for _, peer in xs:
        send(3, c_send, c_recv.at[x], peer)
    c_recv[x] = chunk
    arrived(3, c_recv, SIDE - 1)

    chunk = total(c_recv, SIDE)
    d_send[...] = chunk
    for _, peer in ys:
        send(4, d_send, d_recv.at[y], peer, slot_sem.at[y])
    d_recv[y] = chunk
    acc = jnp.zeros((16, 2 * TOK), F32)
    for k in [y] + [k for k, _ in reversed(ys)]:
        if k is not y:
            pltpu.make_async_copy(d_recv.at[k], d_recv.at[k], slot_sem.at[k]).wait()
        at = pl.ds(pl.multiple_of(k * DCH, DCH), DCH)
        part = d_recv[k] - gb[:, at]
        lf[:, at] = part
        part = jnp.concatenate([*pieces(part), jnp.zeros((16 - 3 * OWN, DCH), F32)], axis=0).astype(BF16)
        lp[:, at] = part
        acc = acc + nt_dot(part, xub[: 2 * TOK, at])
    acc = acc[:OWN] + acc[OWN : 2 * OWN] + acc[2 * OWN : 3 * OWN]

    my_lanes = pl.ds(pl.multiple_of(dp // 2 * 128, 128), 128)
    own = lf[:, my_lanes]
    tile = jnp.concatenate([acc[:, :TOK] * (mask * inv_live), acc[:, TOK:] * INV_TOKENS, own, own], axis=0)
    g_send[...] = tile
    for _, peer in ts:
        send(5, g_send, g_recv.at[t], peer)
    g_recv[t] = tile
    own = nt_dot(lp[...], xub[2 * TOK :, :])
    own = own[:OWN] + own[OWN : 2 * OWN] + own[2 * OWN : 3 * OWN]
    h_send[...] = own
    for _, peer in ts:
        send(12, h_send, h_recv.at[t], peer)
    h_recv[t] = own
    arrived(5, g_recv, NT - 1)
    for k in range(NT):
        tile = g_recv[k]
        at = slice(OWN * k, OWN * (k + 1))
        back[at, :128] = tile[:2]
        back[at, 128:] = tile[2:4]
        mine[at, :] = tile[4:6]

    stacked = jnp.concatenate(pieces(back[...]), axis=0).astype(BF16)

    def right_part(first, width):
        part = jnp.dot(stacked, yvw[: 2 * TOK, pl.ds(first, width)], preferred_element_type=F32)
        return part[:RANK] + part[RANK : 2 * RANK] + part[2 * RANK :]

    for k in range(0, SIDE, 2):
        part = right_part(k * 128, 256)
        ea_send[k] = part[:, :128]
        ea_send[k + 1] = part[:, 128:]
    for k, peer in ys:
        send(6, ea_send.at[k], ea_recv.at[y], peer)
    for h in range(2):
        part = right_part(ACOLS + h * BCOLS, BCOLS)
        for k in range(RANK // 8):
            eb_send[2 * k + h] = part[8 * k : 8 * (k + 1)]
    for k, peer in xs:
        send(7, eb_send.at[k], eb_recv.at[x], peer)
    ea_recv[y] = ea_send[y]
    eb_recv[x] = eb_send[x]
    half = lax.rem(dp, 2)
    lanes = lax.broadcasted_iota(jnp.int32, (RANK, 128), 1)
    my_rows = jnp.where(lanes // 64 == half, mine[...], 0.0)
    gram = dot32(my_rows, my_rows, ((1,), (1,)))
    gram = jnp.concatenate([gram[8 * k : 8 * (k + 1)] for k in range(RANK // 8)], axis=1)
    p_send[...] = gram
    for _, peer in xs:
        send(13, p_send, p_recv.at[x], peer)
    p_recv[x] = gram
    arrived(12, h_recv, NT - 1)
    for k in range(NT):
        crs[OWN * k : OWN * (k + 1), :] = h_recv[k]
    cross = crs[:, :RANK] + crs[:, RANK : 2 * RANK] + crs[:, 2 * RANK : 3 * RANK]
    cw[...] = dot32(cross, wt[...])
    arrived(7, eb_recv, SIDE - 1)
    part = total(eb_recv, SIDE)
    fb_send[...] = part
    for _, peer in ys:
        send(9, fb_send, fb_recv.at[y], peer)
    fb_recv[y] = part
    arrived(6, ea_recv, SIDE - 1)
    part = total(ea_recv, SIDE)
    fa_send[...] = part
    for _, peer in xs:
        send(8, fa_send, fa_recv.at[x], peer)
    fa_recv[x] = part
    arrived(13, p_recv, SIDE - 1)
    gram = total(p_recv, SIDE)
    q_send[...] = gram
    for _, peer in ys:
        send(14, q_send, q_recv.at[y], peer)
    q_recv[y] = gram
    arrived(9, fb_recv, SIDE - 1)
    part = total(fb_recv, SIDE)
    gb_send[...] = part
    for _, peer in xs:
        send(11, gb_send, gb_recv.at[x], peer)
    gb_recv[x] = part
    arrived(8, fa_recv, SIDE - 1)
    part = total(fa_recv, SIDE)
    ga_send[...] = part
    for _, peer in ys:
        send(10, ga_send, ga_recv.at[y], peer)
    ga_recv[y] = part
    arrived(14, q_recv, SIDE - 1)
    packed = total(q_recv, SIDE)
    gram = jnp.concatenate([packed[:, RANK * k : RANK * (k + 1)] for k in range(RANK // 8)], axis=0)
    inverse = inverse_factor(gram)
    basis = dot32(inverse, mine[...])
    rows = dot32(basis, inverse, ((0,), (0,)))
    rows = jnp.where(half == 0, rows[:64], rows[64:])
    high, mid, low = pieces(jnp.concatenate([inverse, rows], axis=0))
    both = jnp.concatenate([high, high, mid, high, mid, low], axis=1).astype(BF16)

    def finish(first, raw):
        width = raw.shape[1]
        high, mid, low = pieces(raw - cw[:, first : first + width])
        right = jnp.concatenate([high, mid, high, low, mid, high], axis=0).astype(BF16)
        out = jnp.dot(both, right, preferred_element_type=F32)
        nxt_ref[:, first : first + width] = out[:RANK]
        upd_ref[:, first : first + width] = out[RANK:].astype(BF16)

    arrived(11, gb_recv, SIDE - 1)
    for h in range(2):
        finish(ACOLS + h * BCOLS, jnp.concatenate([gb_recv[2 * k + h] for k in range(RANK // 8)], axis=0))
    arrived(10, ga_recv, SIDE - 1)
    for k in range(0, SIDE, 2):
        finish(k * 128, jnp.concatenate([ga_recv[k], ga_recv[k + 1]], axis=1))

    for phase, (ref, count) in enumerate(
        (
            (a_recv, NT - 1), (l_recv, SIDE - 1), (b_recv, SIDE - 1), (c_recv, SIDE - 1), (d_recv, SIDE - 1), (g_recv, NT - 1),
            (ea_recv, SIDE - 1), (eb_recv, SIDE - 1), (fa_recv, SIDE - 1), (fb_recv, SIDE - 1), (ga_recv, SIDE - 1), (gb_recv, SIDE - 1),
            (h_recv, NT - 1), (p_recv, SIDE - 1), (q_recv, SIDE - 1),
        )
    ):
        left(phase, ref, count)


def shards(activations, out_grads, token_ids, prev_acts, prev_grads, prev_basis, warm_start):
    def vmem(*shape, dtype=F32):
        return pltpu.VMEM(shape, dtype)

    operands = (activations, out_grads, token_ids.reshape(1, TOK), prev_acts, prev_grads, prev_basis.T, warm_start.T)
    hbm = pl.BlockSpec(memory_space=pltpu.HBM)
    local = pl.BlockSpec(memory_space=pltpu.VMEM)
    update, start = pl.pallas_call(
        kernel,
        out_shape=(jax.ShapeDtypeStruct((DIM // REPLICAS, FF), BF16), jax.ShapeDtypeStruct((RANK, FF), F32)),
        in_specs=[hbm] * 7,
        out_specs=(local, local),
        scratch_shapes=[
            vmem(3 * TOK, DIM, dtype=BF16), vmem(3 * TOK, FF, dtype=BF16), vmem(RANK, DIM), vmem(RANK, FF),
            vmem(NT, 8, 128), vmem(NT, 8, 128), vmem(1, 128), vmem(SIDE, 1, 128),
            vmem(SIDE, 2 * OWN, DCH + 128), vmem(SIDE, 2 * OWN, DCH + 128),
            vmem(OWN, DCH), vmem(SIDE, OWN, DCH), vmem(OWN, DCH), vmem(SIDE, OWN, DCH),
            vmem(OWN, DIM), vmem(OWN, DIM), vmem(8, 128), vmem(NT, 8, 128),
            vmem(RANK, 2 * TOK), vmem(RANK, 128), vmem(RANK, 128), vmem(RANK, FF),
            vmem(SIDE, RANK, 128), vmem(SIDE, RANK, 128), vmem(SIDE, 8, BCOLS), vmem(SIDE, 8, BCOLS),
            vmem(RANK, 128), vmem(SIDE, RANK, 128), vmem(8, BCOLS), vmem(SIDE, 8, BCOLS),
            vmem(RANK, 128), vmem(SIDE, RANK, 128), vmem(8, BCOLS), vmem(SIDE, 8, BCOLS),
            vmem(OWN, 128), vmem(NT, OWN, 128), vmem(8, 128), vmem(SIDE, 8, 128), vmem(8, 128), vmem(SIDE, 8, 128), vmem(16, DIM, dtype=BF16),
            vmem(1, TOK, dtype=jnp.int32), pltpu.SemaphoreType.DMA((7,)), pltpu.SemaphoreType.DMA((15,)),
            pltpu.SemaphoreType.DMA((15,)), pltpu.SemaphoreType.DMA((SIDE,)),
        ],
        compiler_params=pltpu.CompilerParams(collective_id=0, has_side_effects=True, vmem_limit_bytes=40 * 2**20),
        cost_estimate=pl.CostEstimate(flops=10**9, bytes_accessed=5 * 10**6, transcendentals=0),
    )(*(pltpu.with_memory_space_constraint(a, pltpu.HBM) for a in operands))
    return update, start.T


def solution(mesh):
    in_specs = (P("dp", None), P("dp", "tensor"), P("dp"), P("dp", None), P("dp", "tensor"), P(), P("tensor", None))
    out_specs = (P("dp", "tensor"), P("tensor", None))
    return jax.shard_map(shards, mesh=mesh, in_specs=in_specs, out_specs=out_specs, check_vma=False)
```

```python
import jax
import jax.numpy as jnp
from jax import lax
from jax.experimental import pallas as pl
from jax.experimental.pallas import tpu as pltpu
from jax.sharding import PartitionSpec as P

MESH = pl.DeviceIdType.MESH
F32, BF16 = jnp.float32, jnp.bfloat16
HIGHEST = lax.Precision.HIGHEST

SIDE = 8
NT = 16
REPLICAS = 64
TOK = 128
RANK = 32
OWN = RANK // NT
DIM = 4096
FF = 1792
DCH = DIM // SIDE
FAR = (4, 3, 5, 2, 6, 1, 7)
INV_TOKENS = 1.0 / (REPLICAS * TOK)
ACOLS = 1024
BCOLS = 384


def nt_dot(first, second):
    return lax.dot_general(first, second, (((1,), (1,)), ((), ())), preferred_element_type=F32)


def dot32(first, second, dims=((1,), (0,))):
    return lax.dot_general(first, second, (dims, ((), ())), precision=HIGHEST, preferred_element_type=F32)


def pieces(value):
    high = value.astype(BF16).astype(F32)
    rest = value - high
    mid = rest.astype(BF16).astype(F32)
    low = (rest - mid).astype(BF16).astype(F32)
    return high, mid, low


def total(ref, count):
    acc = ref[0]
    for k in range(1, count):
        acc = acc + ref[k]
    return acc


def inverse_factor(gram):
    rows = lax.broadcasted_iota(jnp.int32, (RANK, 128), 0)
    lanes = lax.broadcasted_iota(jnp.int32, (RANK, 128), 1)
    eye = (lanes == rows + RANK).astype(F32)
    work = jnp.concatenate([gram, jnp.zeros((RANK, 128 - RANK), F32)], axis=1) + eye
    for k in range(RANK):
        row = work[k : k + 1, :]
        pivot = row[:, k : k + 1]
        column = work[:, k : k + 1]
        scaled = row * (1.0 / pivot)
        root = row * lax.rsqrt(pivot)
        below = work - column * scaled
        work = jnp.where(rows > k, below, jnp.where(rows == k, root, work))
    return work[:, RANK : 2 * RANK]


def kernel(
    x_hbm, y_hbm, ids_hbm, u_hbm, v_hbm, bt_hbm, wt_hbm,
    upd_ref, nxt_ref,
    xub, yvw, bt, wt,
    a_send, a_recv, l_send, l_recv, b_send, b_recv, c_send, c_recv, d_send, d_recv,
    gb, lf, g_send, g_recv, back, mine, crs, cw,
    ea_send, ea_recv, eb_send, eb_recv, fa_send, fa_recv, fb_send, fb_recv,
    ga_send, ga_recv, gb_send, gb_recv,
    h_send, h_recv, p_send, p_recv, q_send, q_recv, lp,
    ids, load_sem, send_sem, recv_sem, slot_sem,
):
    dp, t = lax.axis_index("dp"), lax.axis_index("tensor")
    y, x = dp // SIDE, lax.rem(dp, SIDE)
    z, core = t // 2, lax.rem(t, 2)

    ring = [lax.rem(jnp.int32(k) + x, SIDE) for k in FAR]
    xs = [(k, (y * SIDE + k, t)) for k in ring]
    ring = [lax.rem(jnp.int32(k) + y, SIDE) for k in FAR]
    ys = [(k, (k * SIDE + x, t)) for k in ring]
    ts = []
    for k in FAR:
        zk = lax.rem(z + k, SIDE)
        ts += [(zk * 2, (dp, zk * 2)), (zk * 2 + 1, (dp, zk * 2 + 1))]
    ts.append((t + 1 - 2 * core, (dp, t + 1 - 2 * core)))

    barrier = pltpu.get_barrier_semaphore()
    for _, peer in ts + ys + xs:
        pl.semaphore_signal(barrier, inc=1, device_id=peer, device_id_type=MESH)

    loads = []
    for k, (src, dst) in enumerate(
        (
            (wt_hbm, wt),
            (y_hbm, yvw.at[pl.ds(0, TOK)]),
            (v_hbm, yvw.at[pl.ds(TOK, TOK)]),
            (bt_hbm, bt),
            (x_hbm, xub.at[pl.ds(0, TOK)]),
            (u_hbm, xub.at[pl.ds(TOK, TOK)]),
            (ids_hbm, ids),
        )
    ):
        copy = pltpu.make_async_copy(src, dst, load_sem.at[k])
        copy.start()
        loads.append(copy)

    def send(phase, src, dst, peer, sem=None):
        sem = recv_sem.at[phase] if sem is None else sem
        pltpu.make_async_remote_copy(
            src_ref=src, dst_ref=dst, send_sem=send_sem.at[phase], recv_sem=sem, device_id=peer, device_id_type=MESH
        ).start()

    def arrived(phase, ref, count):
        whole = ref.at[pl.ds(0, count)]
        pltpu.make_async_copy(whole, whole, recv_sem.at[phase]).wait()

    def left(phase, ref, count):
        whole = ref.at[pl.ds(0, count)]
        pltpu.make_async_copy(whole, whole, send_sem.at[phase]).wait()

    loads[6].wait()
    mask = (ids[...] != 0).astype(F32)
    l_send[...] = jnp.broadcast_to(jnp.sum(mask, axis=1, keepdims=True), (1, 128))
    loads[0].wait()
    for k, piece in enumerate(pieces(wt[...])):
        yvw[2 * TOK + k * RANK : 2 * TOK + (k + 1) * RANK, :] = piece.astype(BF16)
    yvw[2 * TOK + 3 * RANK :, :] = jnp.zeros((RANK, FF), BF16)
    loads[1].wait()
    loads[2].wait()
    proj = nt_dot(yvw[2 * TOK : 2 * TOK + 3 * RANK, :], yvw[...])
    proj = proj[:RANK] + proj[RANK : 2 * RANK] + proj[2 * RANK :]
    for k in range(NT):
        own = proj[OWN * k : OWN * (k + 1)]
        a_send[k] = jnp.concatenate([own[:, :128], own[:, 128:256], own[:, 256:], own[:, 256:]], axis=0)
    pl.semaphore_wait(barrier, len(ts + ys + xs))

    for k, peer in ts:
        send(0, a_send.at[k], a_recv.at[t], peer)
    for _, peer in xs:
        send(1, l_send, l_recv.at[x], peer)
    a_recv[t] = a_send[t]
    l_recv[x] = l_send[...]
    loads[3].wait()
    for k, piece in enumerate(pieces(bt[...])):
        xub[2 * TOK + k * RANK : 2 * TOK + (k + 1) * RANK, :] = piece.astype(BF16)
    xub[2 * TOK + 3 * RANK :, :] = jnp.zeros((RANK, DIM), BF16)
    loads[4].wait()
    loads[5].wait()
    arrived(0, a_recv, NT - 1)
    own = total(a_recv, NT)
    rows = lax.broadcasted_iota(jnp.int32, (2 * OWN, TOK), 0)
    now = jnp.where(rows < OWN, own[: 2 * OWN] * mask, 0.0)
    old = jnp.where(rows >= OWN, own[: 2 * OWN] * INV_TOKENS, 0.0)
    stacked = jnp.concatenate([now, old], axis=1)
    stacked = jnp.concatenate([*pieces(stacked), jnp.zeros((2 * OWN, 2 * TOK), F32)], axis=0).astype(BF16)
    arrived(1, l_recv, SIDE - 1)
    live_x = jnp.broadcast_to(total(l_recv, SIDE), (2 * OWN, 128))

    def left_chunk(k):
        part = jnp.dot(stacked, xub[: 2 * TOK, pl.ds(pl.multiple_of(k * DCH, DCH), DCH)], preferred_element_type=F32)
        return part[: 2 * OWN] + part[2 * OWN : 4 * OWN] + part[4 * OWN : 6 * OWN]

    for k, peer in ys:
        b_send[k, :, :DCH] = left_chunk(k)
        b_send[k, :, DCH:] = live_x
        send(2, b_send.at[k], b_recv.at[y], peer)
    b_recv[y, :, :DCH] = left_chunk(y)
    b_recv[y, :, DCH:] = live_x
    square = own[4:6, :RANK] + own[4:6, RANK : 2 * RANK] + own[4:6, 2 * RANK : 3 * RANK]
    gb[...] = dot32(square, bt[...])
    arrived(2, b_recv, SIDE - 1)
    summed = total(b_recv, SIDE)
    inv_live = 1.0 / summed[:1, DCH : DCH + 128]
    inv_wide = jnp.concatenate([inv_live] * (DCH // 128), axis=1)
    chunk = summed[:OWN, :DCH] * inv_wide + summed[OWN:, :DCH]
    c_send[...] = chunk
    for _, peer in xs:
        send(3, c_send, c_recv.at[x], peer)
    c_recv[x] = chunk
    arrived(3, c_recv, SIDE - 1)

    chunk = total(c_recv, SIDE)
    d_send[...] = chunk
    for _, peer in ys:
        send(4, d_send, d_recv.at[y], peer, slot_sem.at[y])
    d_recv[y] = chunk
    acc = jnp.zeros((16, 2 * TOK), F32)
    for k in [y] + [k for k, _ in reversed(ys)]:
        if k is not y:
            pltpu.make_async_copy(d_recv.at[k], d_recv.at[k], slot_sem.at[k]).wait()
        at = pl.ds(pl.multiple_of(k * DCH, DCH), DCH)
        part = d_recv[k] - gb[:, at]
        lf[:, at] = part
        part = jnp.concatenate([*pieces(part), jnp.zeros((16 - 3 * OWN, DCH), F32)], axis=0).astype(BF16)
        lp[:, at] = part
        acc = acc + nt_dot(part, xub[: 2 * TOK, at])
    acc = acc[:OWN] + acc[OWN : 2 * OWN] + acc[2 * OWN : 3 * OWN]

    my_lanes = pl.ds(pl.multiple_of(dp // 2 * 128, 128), 128)
    own = lf[:, my_lanes]
    tile = jnp.concatenate([acc[:, :TOK] * (mask * inv_live), acc[:, TOK:] * INV_TOKENS, own, own], axis=0)
    g_send[...] = tile
    for _, peer in ts:
        send(5, g_send, g_recv.at[t], peer)
    g_recv[t] = tile
    own = nt_dot(lp[...], xub[2 * TOK :, :])
    own = own[:OWN] + own[OWN : 2 * OWN] + own[2 * OWN : 3 * OWN]
    h_send[...] = own
    for _, peer in ts:
        send(12, h_send, h_recv.at[t], peer)
    h_recv[t] = own
    arrived(5, g_recv, NT - 1)
    for k in range(NT):
        tile = g_recv[k]
        at = slice(OWN * k, OWN * (k + 1))
        back[at, :128] = tile[:2]
        back[at, 128:] = tile[2:4]
        mine[at, :] = tile[4:6]

    stacked = jnp.concatenate(pieces(back[...]), axis=0).astype(BF16)

    def right_part(first, width):
        part = jnp.dot(stacked, yvw[: 2 * TOK, pl.ds(first, width)], preferred_element_type=F32)
        return part[:RANK] + part[RANK : 2 * RANK] + part[2 * RANK :]

    for k in range(0, SIDE, 2):
        part = right_part(k * 128, 256)
        ea_send[k] = part[:, :128]
        ea_send[k + 1] = part[:, 128:]
    for k, peer in ys:
        send(6, ea_send.at[k], ea_recv.at[y], peer)
    for h in range(2):
        part = right_part(ACOLS + h * BCOLS, BCOLS)
        for k in range(RANK // 8):
            eb_send[2 * k + h] = part[8 * k : 8 * (k + 1)]
    for k, peer in xs:
        send(7, eb_send.at[k], eb_recv.at[x], peer)
    ea_recv[y] = ea_send[y]
    eb_recv[x] = eb_send[x]
    half = lax.rem(dp, 2)
    lanes = lax.broadcasted_iota(jnp.int32, (RANK, 128), 1)
    my_rows = jnp.where(lanes // 64 == half, mine[...], 0.0)
    gram = dot32(my_rows, my_rows, ((1,), (1,)))
    gram = jnp.concatenate([gram[8 * k : 8 * (k + 1)] for k in range(RANK // 8)], axis=1)
    p_send[...] = gram
    for _, peer in xs:
        send(13, p_send, p_recv.at[x], peer)
    p_recv[x] = gram
    arrived(12, h_recv, NT - 1)
    for k in range(NT):
        crs[OWN * k : OWN * (k + 1), :] = h_recv[k]
    cross = crs[:, :RANK] + crs[:, RANK : 2 * RANK] + crs[:, 2 * RANK : 3 * RANK]
    cw[...] = dot32(cross, wt[...])
    arrived(7, eb_recv, SIDE - 1)
    part = total(eb_recv, SIDE)
    fb_send[...] = part
    for _, peer in ys:
        send(9, fb_send, fb_recv.at[y], peer)
    fb_recv[y] = part
    arrived(6, ea_recv, SIDE - 1)
    part = total(ea_recv, SIDE)
    fa_send[...] = part
    for _, peer in xs:
        send(8, fa_send, fa_recv.at[x], peer)
    fa_recv[x] = part
    arrived(13, p_recv, SIDE - 1)
    gram = total(p_recv, SIDE)
    q_send[...] = gram
    for _, peer in ys:
        send(14, q_send, q_recv.at[y], peer)
    q_recv[y] = gram
    arrived(9, fb_recv, SIDE - 1)
    part = total(fb_recv, SIDE)
    gb_send[...] = part
    for _, peer in xs:
        send(11, gb_send, gb_recv.at[x], peer)
    gb_recv[x] = part
    arrived(8, fa_recv, SIDE - 1)
    part = total(fa_recv, SIDE)
    ga_send[...] = part
    for _, peer in ys:
        send(10, ga_send, ga_recv.at[y], peer)
    ga_recv[y] = part
    arrived(14, q_recv, SIDE - 1)
    packed = total(q_recv, SIDE)
    gram = jnp.concatenate([packed[:, RANK * k : RANK * (k + 1)] for k in range(RANK // 8)], axis=0)
    inverse = inverse_factor(gram)
    basis = dot32(inverse, mine[...])
    rows = dot32(basis, inverse, ((0,), (0,)))
    rows = jnp.where(half == 0, rows[:64], rows[64:])
    high, mid, low = pieces(jnp.concatenate([inverse, rows], axis=0))
    both = jnp.concatenate([high, high, mid, high, mid, low], axis=1).astype(BF16)

    def finish(first, raw):
        width = raw.shape[1]
        high, mid, low = pieces(raw - cw[:, first : first + width])
        right = jnp.concatenate([high, mid, high, low, mid, high], axis=0).astype(BF16)
        out = jnp.dot(both, right, preferred_element_type=F32)
        nxt_ref[:, first : first + width] = out[:RANK]
        upd_ref[:, first : first + width] = out[RANK:].astype(BF16)

    arrived(11, gb_recv, SIDE - 1)
    for h in range(2):
        finish(ACOLS + h * BCOLS, jnp.concatenate([gb_recv[2 * k + h] for k in range(RANK // 8)], axis=0))
    arrived(10, ga_recv, SIDE - 1)
    for k in range(0, SIDE, 2):
        finish(k * 128, jnp.concatenate([ga_recv[k], ga_recv[k + 1]], axis=1))

    for phase, (ref, count) in enumerate(
        (
            (a_recv, NT - 1), (l_recv, SIDE - 1), (b_recv, SIDE - 1), (c_recv, SIDE - 1), (d_recv, SIDE - 1), (g_recv, NT - 1),
            (ea_recv, SIDE - 1), (eb_recv, SIDE - 1), (fa_recv, SIDE - 1), (fb_recv, SIDE - 1), (ga_recv, SIDE - 1), (gb_recv, SIDE - 1),
            (h_recv, NT - 1), (p_recv, SIDE - 1), (q_recv, SIDE - 1),
        )
    ):
        left(phase, ref, count)


def write_out(upd_ref, nxt_ref, upd_out, nxt_out, sem):
    copies = [pltpu.make_async_copy(upd_ref, upd_out, sem.at[0]), pltpu.make_async_copy(nxt_ref, nxt_out, sem.at[1])]
    for copy in copies:
        copy.start()
    for copy in copies:
        copy.wait()


def shards(activations, out_grads, token_ids, prev_acts, prev_grads, prev_basis, warm_start):
    def vmem(*shape, dtype=F32):
        return pltpu.VMEM(shape, dtype)

    operands = (activations, out_grads, token_ids.reshape(1, TOK), prev_acts, prev_grads, prev_basis.T, warm_start.T)
    hbm = pl.BlockSpec(memory_space=pltpu.HBM)
    local = pl.BlockSpec(memory_space=pltpu.VMEM)
    update, start = pl.pallas_call(
        kernel,
        out_shape=(jax.ShapeDtypeStruct((DIM // REPLICAS, FF), BF16), jax.ShapeDtypeStruct((RANK, FF), F32)),
        in_specs=[hbm] * 7,
        out_specs=(local, local),
        scratch_shapes=[
            vmem(3 * TOK, DIM, dtype=BF16), vmem(3 * TOK, FF, dtype=BF16), vmem(RANK, DIM), vmem(RANK, FF),
            vmem(NT, 8, 128), vmem(NT, 8, 128), vmem(1, 128), vmem(SIDE, 1, 128),
            vmem(SIDE, 2 * OWN, DCH + 128), vmem(SIDE, 2 * OWN, DCH + 128),
            vmem(OWN, DCH), vmem(SIDE, OWN, DCH), vmem(OWN, DCH), vmem(SIDE, OWN, DCH),
            vmem(OWN, DIM), vmem(OWN, DIM), vmem(8, 128), vmem(NT, 8, 128),
            vmem(RANK, 2 * TOK), vmem(RANK, 128), vmem(RANK, 128), vmem(RANK, FF),
            vmem(SIDE, RANK, 128), vmem(SIDE, RANK, 128), vmem(SIDE, 8, BCOLS), vmem(SIDE, 8, BCOLS),
            vmem(RANK, 128), vmem(SIDE, RANK, 128), vmem(8, BCOLS), vmem(SIDE, 8, BCOLS),
            vmem(RANK, 128), vmem(SIDE, RANK, 128), vmem(8, BCOLS), vmem(SIDE, 8, BCOLS),
            vmem(OWN, 128), vmem(NT, OWN, 128), vmem(8, 128), vmem(SIDE, 8, 128), vmem(8, 128), vmem(SIDE, 8, 128), vmem(16, DIM, dtype=BF16),
            vmem(1, TOK, dtype=jnp.int32), pltpu.SemaphoreType.DMA((7,)), pltpu.SemaphoreType.DMA((15,)),
            pltpu.SemaphoreType.DMA((15,)), pltpu.SemaphoreType.DMA((SIDE,)),
        ],
        compiler_params=pltpu.CompilerParams(collective_id=0, has_side_effects=True, vmem_limit_bytes=40 * 2**20),
        cost_estimate=pl.CostEstimate(flops=10**9, bytes_accessed=5 * 10**6, transcendentals=0),
    )(*(pltpu.with_memory_space_constraint(a, pltpu.HBM) for a in operands))
    update, start = pl.pallas_call(
        write_out,
        out_shape=(jax.ShapeDtypeStruct(update.shape, BF16), jax.ShapeDtypeStruct(start.shape, F32)),
        in_specs=[local, local],
        out_specs=(hbm, hbm),
        scratch_shapes=[pltpu.SemaphoreType.DMA((2,))],
    )(*(pltpu.with_memory_space_constraint(a, pltpu.VMEM) for a in (update, start)))
    return update, start.T


def solution(mesh):
    in_specs = (P("dp", None), P("dp", "tensor"), P("dp"), P("dp", None), P("dp", "tensor"), P(), P("tensor", None))
    out_specs = (P("dp", "tensor"), P("tensor", None))
    return jax.shard_map(shards, mesh=mesh, in_specs=in_specs, out_specs=out_specs, check_vma=False)
```
